32 devices in a mesh: dp: 4 (over x, core), code: 8 (over z, y).
Axes of the slice: x: 2, y: 2, z: 4, core: 2. Of those that a mesh axis runs over, the one named last changes fastest.
Arguments:
- latents: bfloat16 [2048, 256], P(('dp', 'code')), may hold values from -1000 to 1000
- out_grad: bfloat16 [2048, 256], P(('dp', 'code')), may hold values from -6 to 6
- targets: int32 [2048], P('dp'), may hold values from 0 to 65535
- codebook: bfloat16 [65536, 256], P('code'), may hold values from -2 to 2
Outputs:
- latent_grad: bfloat16 [2048, 256], P(('dp', 'code'))
- codebook_grad: float32 [65536, 256], P(('code', 'dp'))
- token_loss: float32 [2048], P(('dp', 'code'))
The draws below stay inside these ranges and needn't reach their ends.
All inputs are finite; a program needn't handle non-finite values.
Results may differ from the reference program's by a relative error of at most 0.0042.
Values may be sent and summed in bfloat16 or wider, within the bound.
A program may use at most 128 MiB of HBM per device.

```python
import jax
import jax.numpy as jnp
from jax import lax

D = 256
CODE_DEV = 8192
TOK_DEV = 512
TOKENS = 2048
CODES = 65536
N_DP = 4
N_CODE = 8


def shared_book(key):
    base_key = jax.random.fold_in(key, 11)
    entries = jax.random.normal(base_key, (CODES, D), jnp.float32) * D ** (-0.5)
    entries = jnp.clip(entries, -6.0 * D ** (-0.5), 6.0 * D ** (-0.5))
    return entries


def draw_codebook(key, part):
    return shared_book(key).astype(jnp.bfloat16)


def draw_latents(key, part):
    own_key = jax.random.fold_in(key, 12)
    values = jnp.clip(jax.random.normal(own_key, (TOKENS, D), jnp.float32) * 3.0, -18.0, 18.0)
    return values.astype(jnp.bfloat16)


def with_ends(drawn, key, least, high):
    longest = drawn.shape.index(max(drawn.shape))
    spots = []
    for shift in (0, 1):
        where = [jax.random.randint(jax.random.fold_in(key, axis), (), 0, length) for axis, length in enumerate(drawn.shape)]
        where[longest] = (where[longest] + shift) % drawn.shape[longest]
        spots.append(tuple(where))
    return drawn.at[spots[0]].set(least).at[spots[1]].set(high)


def block_levels(rng, shape, cuts, low, top_value):
    def one(position, blocks):
        steps = jax.random.uniform(jax.random.fold_in(jax.random.fold_in(rng, 6), position), (blocks,), jnp.float32, low / len(cuts), top_value / len(cuts))
        return jnp.repeat(jnp.exp(steps), shape[position] // blocks).reshape((-1,) + (1,) * (len(shape) - position - 1))

    factor_of = one(*cuts[0])
    for cut in cuts[1:]:
        factor_of = factor_of * one(*cut)
    return factor_of


def gaussian(key, dims, width, most, cuts=(), kind=jnp.bfloat16):
    loudness = block_levels(key, dims, cuts, -0.22, 0.18) if cuts else 1.0
    values = jax.random.normal(key, dims, jnp.float32) * width * loudness
    return jnp.minimum(jnp.maximum(values, -most), most).astype(kind)


def setup_inputs(seed: int = 0) -> dict:
    arg_keys = jax.random.split(jax.random.key(seed), 5)
    return {
        "latents": draw_latents(jax.random.fold_in(arg_keys[4], 71), 0),
        "out_grad": gaussian(arg_keys[1], (TOKENS, D), 1.0, 6.0, ((0, 32),)),
        "targets": with_ends(jax.random.randint(arg_keys[2], (TOKENS,), 0, CODES), jax.random.fold_in(arg_keys[2], 1), 0, CODES - 1).astype(jnp.int32),
        "codebook": draw_codebook(jax.random.fold_in(arg_keys[4], 71), 0),
    }


ce_weight = 1.0


def reference(latents, out_grad, targets, codebook):
    hi = lax.Precision.HIGHEST
    lat_f = latents.astype(jnp.float32)
    grad_f = out_grad.astype(jnp.float32)
    book_f = codebook.astype(jnp.float32).reshape(N_CODE, CODE_DEV, D)
    offsets = jnp.arange(N_CODE, dtype=jnp.int32) * CODE_DEV

    def scores(book_block):
        return (jnp.dot(lat_f, book_block.T, precision=hi), jnp.dot(grad_f, book_block.T, precision=hi))

    def first_pass(carry, item):
        top, total, weighted, picked = carry
        book_block, offset = item
        logit_block, back_block = scores(book_block)
        new_top = jnp.maximum(top, jnp.max(logit_block, axis=1))
        factor = jnp.exp(top - new_top)
        expo = jnp.exp(logit_block - new_top[:, None])
        code_ids = offset + jnp.arange(CODE_DEV, dtype=jnp.int32)
        hit_mask = targets[:, None] == code_ids[None, :]
        total = total * factor + jnp.sum(expo, axis=1)
        weighted = weighted * factor + jnp.sum(expo * back_block, axis=1)
        picked = picked + jnp.sum(jnp.where(hit_mask, logit_block, 0.0), axis=1)
        return (new_top, total, weighted, picked), None

    zeros_tok = jnp.zeros((TOKENS,), jnp.float32)
    start = (jnp.full((TOKENS,), -jnp.inf, jnp.float32), zeros_tok, zeros_tok, zeros_tok)
    (top, total, weighted, picked), _ = lax.scan(first_pass, start, (book_f, offsets))
    lse = top + jnp.log(total)
    mean_back = weighted / total
    token_loss = lse - picked

    def second_pass(carry, item):
        book_block, offset = item
        logit_block, back_block = scores(book_block)
        probs = jnp.exp(logit_block - lse[:, None])
        code_ids = offset + jnp.arange(CODE_DEV, dtype=jnp.int32)
        onehot = (targets[:, None] == code_ids[None, :]).astype(jnp.float32)
        delta = probs * (back_block - mean_back[:, None]) + ce_weight * (probs - onehot)
        delta = delta.astype(jnp.bfloat16).astype(jnp.float32)
        carry = carry + jnp.dot(delta, book_block, precision=hi)
        delta_groups = delta.reshape(N_DP, TOK_DEV, CODE_DEV)
        onehot_groups = onehot.reshape(N_DP, TOK_DEV, CODE_DEV)
        parts = jnp.einsum("gtk,gtd->gkd", delta_groups, lat_f.reshape(N_DP, TOK_DEV, D), precision=hi)
        parts = parts + jnp.einsum("gtk,gtd->gkd", onehot_groups, grad_f.reshape(N_DP, TOK_DEV, D), precision=hi)
        return carry, jnp.sum(parts, axis=0)

    lat_grad, book_grad = lax.scan(second_pass, jnp.zeros((TOKENS, D), jnp.float32), (book_f, offsets))
    return lat_grad.astype(jnp.bfloat16), book_grad.reshape(CODES, D), token_loss
```

```python
import functools

import jax
import jax.numpy as jnp
from jax import lax
from jax.experimental import pallas as pl
from jax.experimental.pallas import tpu as pltpu
from jax.sharding import PartitionSpec as P

F32 = jnp.float32
BF16 = jnp.bfloat16
CORES = 2


def dims_of(dp, code):
    nx = dp // CORES
    ny = 2 if code % 2 == 0 else 1
    return nx, ny, code // ny


def kernel(
    dims, lat_ref, grad_ref, tgt_ref, book_ref, lg_ref, cg_ref, loss_ref,
    tok, tg, book, book_t, expo, back, delta, tops, sums, stats, stats_in,
    other, other_in, lgrad, lgrad_x, lgrad_y, lgrad_z, acc, ssem, rsem, lsem,
):
    nx, ny, nz, kb = dims
    own, width = lat_ref.shape
    groups = nx * ny
    wide = nz * own
    sub = cg_ref.shape[0]
    codes = CORES * sub
    blocks = codes // kb
    half_blocks = sub // kb
    dp = lax.axis_index("dp")
    code = lax.axis_index("code")
    x, core = dp // CORES, dp % CORES
    z, y = code // ny, code % ny

    def at(dx=0, dy=0, dz=0):
        return (
            lax.rem(x + dx + nx, nx) * CORES + core,
            lax.rem(z + dz + nz, nz) * ny + lax.rem(y + dy + ny, ny),
        )

    mate = (x * CORES + (1 - core), code)
    used = [0]

    def send(src, dst, device):
        i = used[0]
        used[0] += 1
        return pltpu.make_async_remote_copy(
            src_ref=src, dst_ref=dst, send_sem=ssem.at[i], recv_sem=rsem.at[i],
            device_id=device, device_id_type=pl.DeviceIdType.MESH,
        )

    first_code = code * book_ref.shape[0]
    bases = (
        first_code + (x * CORES + (1 - core)) * sub,
        first_code + dp * sub,
    )
    loads = []
    for half, row in enumerate((1 - core, core)):
        start = pl.multiple_of((x * CORES + row) * sub, sub)
        load = pltpu.make_async_copy(
            book_ref.at[pl.ds(start, sub)], book.at[pl.ds(half * sub, sub)], lsem.at[half]
        )
        load.start()
        loads.append(load)

    tok[0:own, 0:width] = lat_ref[...]
    tok[0:own, width:] = grad_ref[...]
    for ry in range(ny):
        tg[ry] = tgt_ref[ry]

    barrier = pltpu.get_barrier_semaphore()
    partners = [at(dx=k) for k in range(1, nx)] + [at(dy=k) for k in range(1, ny)]
    partners += [at(dz=k) for k in range(1, nz)] + [mate]
    for partner in partners:
        pl.semaphore_signal(barrier, inc=1, device_id=partner, device_id_type=pl.DeviceIdType.MESH)
    pl.semaphore_wait(barrier, len(partners))

    def rows(rx, ry, rz):
        return pl.ds(((rx * ny + ry) * nz + rz) * own, own)

    pending = []

    def launch(copy):
        copy.start()
        pending.append(copy)
        return copy

    z_in = {
        k: launch(send(tok.at[rows(0, 0, 0)], tok.at[rows(0, 0, k)], at(dz=-k)))
        for k in range(1, nz)
    }
    x_in, y_in = {}, {}

    def forward_x(ry, rz):
        for k in range(1, nx):
            x_in[k, ry, rz] = launch(
                send(tok.at[rows(0, ry, rz)], tok.at[rows(k, ry, rz)], at(dx=-k))
            )

    def forward_y(rz):
        for k in range(1, ny):
            y_in[k, rz] = launch(
                send(tok.at[rows(0, 0, rz)], tok.at[rows(0, k, rz)], at(dy=-k))
            )

    forward_x(0, 0)
    forward_y(0)
    tg_in = {
        k: launch(send(tg.at[pl.ds(0, ny)], tg.at[pl.ds(k * ny, ny)], at(dx=-k)))
        for k in range(1, nx)
    }
    for rz in range(1, nz):
        z_in[rz].wait_recv()
        forward_x(0, rz)
        forward_y(rz)
    for load in loads:
        load.wait()

    nt = (((1,), (1,)), ((), ()))

    def base_of(b):
        return jnp.where(b < half_blocks, bases[0] + b * kb, bases[1] + (b - half_blocks) * kb)

    def hits(g, b):
        ids = lax.broadcasted_iota(jnp.int32, (kb, wide), 0)
        return ids == (tg[g] - base_of(b))

    def first_pass(g):
        lat_g = tok[g * wide : (g + 1) * wide, 0:width]
        grad_g = tok[g * wide : (g + 1) * wide, width:]

        def body(b, carry):
            here = pl.ds(pl.multiple_of(b * kb, kb), kb)
            part = book[here, :]
            logit = lax.dot_general(part, lat_g, nt, preferred_element_type=F32)
            bk = lax.dot_general(part, grad_g, nt, preferred_element_type=F32)
            top = jnp.max(logit, axis=0, keepdims=True)
            ex = jnp.exp(logit - top)
            expo[g, here, :] = ex
            back[g, here, :] = bk
            tops[g, pl.ds(b, 1), :] = top
            sums[0, pl.ds(b, 1), :] = jnp.sum(ex, axis=0, keepdims=True)
            sums[1, pl.ds(b, 1), :] = jnp.sum(ex * bk, axis=0, keepdims=True)
            sums[2, pl.ds(b, 1), :] = jnp.sum(
                jnp.where(hits(g, b), logit, 0.0), axis=0, keepdims=True
            )
            return carry

        lax.fori_loop(0, blocks, body, 0, unroll=2)
        block_tops = tops[g]
        top = jnp.max(block_tops, axis=0, keepdims=True)
        factor = jnp.exp(block_tops - top)
        stats[0, g, 0:1, :] = top
        stats[0, g, 1:2, :] = jnp.sum(sums[0] * factor, axis=0, keepdims=True)
        stats[0, g, 2:3, :] = jnp.sum(sums[1] * factor, axis=0, keepdims=True)
        stats[0, g, 3:4, :] = jnp.sum(sums[2], axis=0, keepdims=True)
        stats[0, g, 4:8, :] = jnp.zeros((4, wide), F32)

    first_pass(0)
    for k in range(1, ny):
        for rz in range(nz):
            y_in[k, rz].wait_recv()
            forward_x(k, rz)
    for ry in range(1, ny):
        first_pass(ry)
    for b in range(blocks):
        book_t[:, b * kb : (b + 1) * kb] = book[b * kb : (b + 1) * kb, :].T
    for k in range(1, nx):
        tg_in[k].wait_recv()
        for ry in range(ny):
            for rz in range(nz):
                x_in[k, ry, rz].wait_recv()
            first_pass(k * ny + ry)

    def merge(mine, theirs):
        top = jnp.maximum(mine[0:1], theirs[0:1])
        fm, ft = jnp.exp(mine[0:1] - top), jnp.exp(theirs[0:1] - top)
        return jnp.concatenate(
            [
                top,
                mine[1:2] * fm + theirs[1:2] * ft,
                mine[2:3] * fm + theirs[2:3] * ft,
                mine[3:4] + theirs[3:4],
                jnp.zeros((4, wide), F32),
            ],
            axis=0,
        )

    def direct_part(lo, hi):
        def body(b, carry):
            here = pl.ds(pl.multiple_of(b * kb, kb), kb)
            total = None
            for g in range(groups):
                onehot = hits(g, b).astype(F32).astype(BF16)
                term = jnp.dot(
                    onehot, tok[g * wide : (g + 1) * wide, width:], preferred_element_type=F32
                )
                total = term if total is None else total + term
            if lo == 0:
                other[here, :] = total
            else:
                cg_ref[pl.ds(pl.multiple_of((b - half_blocks) * kb, kb), kb), :] = total
            return carry

        lax.fori_loop(lo, hi, body, 0)

    slot = 0
    stages = [("x", nx), ("y", ny), ("z", nz)]
    for s, (axis, n) in enumerate(stages):
        arrivals = []
        for k in range(1, n):
            to = at(**{"d" + axis: -k})
            arrivals.append((k, slot, launch(send(stats.at[s], stats_in.at[slot], to))))
            slot += 1
        if s == 0:
            direct_part(0, half_blocks)
        if s == 1:
            direct_part(half_blocks, blocks)
        for _, _, copy in arrivals:
            copy.wait_recv()
        for g in range(groups):
            rx, ry = g // ny, g % ny
            value = stats[s, g]
            for k, place, _ in arrivals:
                if axis == "x":
                    theirs = stats_in[place, ((rx - k) % nx) * ny + ry]
                elif axis == "y":
                    theirs = stats_in[place, rx * ny + (ry - k) % ny]
                else:
                    theirs = pltpu.roll(stats_in[place, g], k * own, 1)
                value = merge(value, theirs)
            stats[s + 1, g] = value
    final = len(stages)
    top = stats[final, 0, 0:1, :]
    loss = top + jnp.log(stats[final, 0, 1:2, :]) - stats[final, 0, 3:4, :]
    loss_ref[...] = loss[:, 0:own]

    def second_pass(g):
        lse = stats[final, g, 0:1, :] + jnp.log(stats[final, g, 1:2, :])
        shift = 1.0 - stats[final, g, 2:3, :] / stats[final, g, 1:2, :]
        acc[...] = jnp.zeros_like(acc)

        def body(b, carry):
            here = pl.ds(pl.multiple_of(b * kb, kb), kb)
            scale = jnp.exp(tops[g, pl.ds(b, 1), :] - lse)
            probs = expo[g, here, :] * scale
            value = probs * (back[g, here, :] + shift)
            value = value - jnp.where(hits(g, b), 1.0, 0.0)
            value = value.astype(BF16)
            delta[here, g * wide : (g + 1) * wide] = value
            acc[...] += jnp.dot(book_t[:, here], value, preferred_element_type=F32)
            return carry

        lax.fori_loop(0, blocks, body, 0, unroll=2)
        lgrad[g * wide : (g + 1) * wide, :] = acc[...].T.astype(BF16)

    lx_in, ly_in, lz_in = {}, {}, {}
    for k in range(1, nx):
        for ry in reversed(range(ny)):
            g = k * ny + ry
            second_pass(g)
            lx_in[k, ry] = launch(
                send(
                    lgrad.at[pl.ds(g * wide, wide)],
                    lgrad_x.at[pl.ds(((k - 1) * ny + ry) * wide, wide)],
                    at(dx=k),
                )
            )
    for ry in reversed(range(ny)):
        second_pass(ry)

    def sum_x(ry):
        value = lgrad[ry * wide : (ry + 1) * wide, :].astype(F32)
        for k in range(1, nx):
            lx_in[k, ry].wait_recv()
            value += lgrad_x[((k - 1) * ny + ry) * wide : ((k - 1) * ny + ry + 1) * wide, :].astype(F32)
        return value

    def book_part(lo, hi, ref):
        def body(b, carry):
            here = pl.ds(pl.multiple_of(b * kb, kb), kb)
            there = pl.ds(pl.multiple_of((b - lo) * kb, kb), kb)
            ref[there, :] += jnp.dot(delta[here, :], tok[:, 0:width], preferred_element_type=F32)
            return carry

        lax.fori_loop(lo, hi, body, 0)

    other_copies = []
    for b in range(half_blocks):
        here = pl.ds(b * kb, kb)
        other[here, :] += jnp.dot(delta[b * kb : (b + 1) * kb, :], tok[:, 0:width], preferred_element_type=F32)
        other_copies.append(launch(send(other.at[here], other_in.at[here], mate)))

    for k in range(1, ny):
        lgrad[k * wide : (k + 1) * wide, :] = sum_x(k).astype(BF16)
        ly_in[k] = launch(
            send(
                lgrad.at[pl.ds(k * wide, wide)],
                lgrad_y.at[pl.ds((k - 1) * wide, wide)],
                at(dy=k),
            )
        )
    mine = sum_x(0)
    acc[...] = mine
    book_part(half_blocks, blocks, cg_ref)

    mine = acc[...]
    for k in range(1, ny):
        ly_in[k].wait_recv()
        mine = mine + lgrad_y[(k - 1) * wide : k * wide, :].astype(F32)
    acc[...] = mine
    lgrad[own:wide, :] = acc[own:wide, :].astype(BF16)
    for k in range(1, nz):
        lz_in[k] = launch(
            send(
                lgrad.at[pl.ds(k * own, own)],
                lgrad_z.at[pl.ds((k - 1) * own, own)],
                at(dz=k),
            )
        )
    for b in range(half_blocks):
        other_copies[b].wait_recv()
        cg_ref[b * kb : (b + 1) * kb, :] += other_in[b * kb : (b + 1) * kb, :]
    mine = acc[0:own, :]
    for k in range(1, nz):
        lz_in[k].wait_recv()
        mine = mine + lgrad_z[(k - 1) * own : k * own, :].astype(F32)
    lg_ref[...] = mine.astype(BF16)
    for copy in pending:
        copy.wait_send()


def per_device(latents, out_grad, targets, codebook):
    own, width = latents.shape
    code_dev = codebook.shape[0]
    dp, code = lax.axis_size("dp"), lax.axis_size("code")
    nx, ny, nz = dims_of(dp, code)
    groups = nx * ny
    wide = nz * own
    sub = code_dev // dp
    codes = CORES * sub
    kb = min(512, sub)
    blocks = codes // kb
    tokens = groups * wide

    place = lax.axis_index("code")
    z, y = place // ny, place % ny
    ordered = targets.reshape(nz, ny, own)
    ordered = lax.dynamic_slice_in_dim(jnp.concatenate([ordered, ordered], 0), z, nz, 0)
    ordered = lax.dynamic_slice_in_dim(jnp.concatenate([ordered, ordered], 1), y, ny, 1)
    ordered = ordered.transpose(1, 0, 2).reshape(ny, 1, wide)

    copies = (nz - 1) + (nx - 1) * (ny * nz + 1) + (ny - 1) * nz
    copies += (nx - 1) + (ny - 1) + (nz - 1)
    copies += (nx - 1) * ny + (ny - 1) + (nz - 1) + sub // kb
    vmem = pl.BlockSpec(memory_space=pltpu.VMEM)
    macs = tokens * codes * width
    lat_out, book_out, loss = pl.pallas_call(
        functools.partial(kernel, (nx, ny, nz, kb)),
        out_shape=(
            jax.ShapeDtypeStruct((own, width), BF16),
            jax.ShapeDtypeStruct((sub, width), F32),
            jax.ShapeDtypeStruct((1, own), F32),
        ),
        in_specs=[vmem, vmem, vmem, pl.BlockSpec(memory_space=pl.ANY)],
        out_specs=(vmem, vmem, vmem),
        scratch_shapes=[
            pltpu.VMEM((tokens, 2 * width), BF16),
            pltpu.VMEM((groups, 1, wide), jnp.int32),
            pltpu.VMEM((codes, width), BF16),
            pltpu.VMEM((width, codes), BF16),
            pltpu.VMEM((groups, codes, wide), F32),
            pltpu.VMEM((groups, codes, wide), F32),
            pltpu.VMEM((codes, tokens), BF16),
            pltpu.VMEM((groups, blocks, wide), F32),
            pltpu.VMEM((3, blocks, wide), F32),
            pltpu.VMEM((4, groups, 8, wide), F32),
            pltpu.VMEM((max(1, nx + ny + nz - 3), groups, 8, wide), F32),
            pltpu.VMEM((sub, width), F32),
            pltpu.VMEM((sub, width), F32),
            pltpu.VMEM((tokens, width), BF16),
            pltpu.VMEM((max(1, nx - 1) * ny * wide, width), BF16),
            pltpu.VMEM((max(1, ny - 1) * wide, width), BF16),
            pltpu.VMEM((max(1, nz - 1) * own, width), BF16),
            pltpu.VMEM((width, wide), F32),
            pltpu.SemaphoreType.DMA((copies,)),
            pltpu.SemaphoreType.DMA((copies,)),
            pltpu.SemaphoreType.DMA((2,)),
        ],
        compiler_params=pltpu.CompilerParams(
            collective_id=0, has_side_effects=True, vmem_limit_bytes=62 * 2**20
        ),
        cost_estimate=pl.CostEstimate(
            flops=10 * macs, bytes_accessed=2 * codes * width, transcendentals=tokens * codes
        ),
    )(latents, out_grad, ordered, codebook)
    return lat_out, book_out, loss.reshape(own)


def solution(mesh):
    in_specs = (P(("dp", "code"), None), P(("dp", "code"), None), P("dp"), P("code", None))
    out_specs = (P(("dp", "code"), None), P(("code", "dp"), None), P(("dp", "code")))
    return jax.shard_map(
        per_device, mesh=mesh, in_specs=in_specs, out_specs=out_specs, check_vma=False
    )
```

```python
import functools

import jax
import jax.numpy as jnp
from jax import lax
from jax.experimental import pallas as pl
from jax.experimental.pallas import tpu as pltpu
from jax.sharding import PartitionSpec as P

F32 = jnp.float32
BF16 = jnp.bfloat16
CORES = 2


def dims_of(dp, code):
    nx = dp // CORES
    ny = 2 if code % 2 == 0 else 1
    return nx, ny, code // ny


def kernel(
    dims, lat_ref, grad_ref, tgt_ref, book_ref, lg_ref, mine_ref, theirs_ref, loss_ref,
    tok, tg, book, book_t, expo, back, delta, tops, sums, stats, stats_in,
    other, same, lgrad, lgrad_x, lgrad_y, lgrad_z, acc, ssem, rsem, lsem,
):
    nx, ny, nz, kb = dims
    own, width = lat_ref.shape
    groups = nx * ny
    wide = nz * own
    sub = mine_ref.shape[0]
    codes = CORES * sub
    blocks = codes // kb
    half_blocks = sub // kb
    dp = lax.axis_index("dp")
    code = lax.axis_index("code")
    x, core = dp // CORES, dp % CORES
    z, y = code // ny, code % ny

    def at(dx=0, dy=0, dz=0):
        return (
            lax.rem(x + dx + nx, nx) * CORES + core,
            lax.rem(z + dz + nz, nz) * ny + lax.rem(y + dy + ny, ny),
        )

    mate = (x * CORES + (1 - core), code)
    used = [0]

    def send(src, dst, device):
        i = used[0]
        used[0] += 1
        return pltpu.make_async_remote_copy(
            src_ref=src, dst_ref=dst, send_sem=ssem.at[i], recv_sem=rsem.at[i],
            device_id=device, device_id_type=pl.DeviceIdType.MESH,
        )

    first_code = code * book_ref.shape[0]
    bases = (
        first_code + (x * CORES + (1 - core)) * sub,
        first_code + dp * sub,
    )
    loads = []
    for half, row in enumerate((1 - core, core)):
        start = pl.multiple_of((x * CORES + row) * sub, sub)
        load = pltpu.make_async_copy(
            book_ref.at[pl.ds(start, sub)], book.at[pl.ds(half * sub, sub)], lsem.at[half]
        )
        load.start()
        loads.append(load)

    tok[0:own, 0:width] = lat_ref[...]
    tok[0:own, width:] = grad_ref[...]
    barrier = pltpu.get_barrier_semaphore()
    square = [(kx, ky) for kx in range(nx) for ky in range(ny)][1:]
    partners = [at(dx=kx, dy=ky) for kx, ky in square]
    partners += [at(dz=k) for k in range(1, nz)] + [mate]
    for partner in partners:
        pl.semaphore_signal(barrier, inc=1, device_id=partner, device_id_type=pl.DeviceIdType.MESH)
    pl.semaphore_wait(barrier, len(partners))

    cut = own // 2 if ny > 1 and own % 32 == 0 else own

    def rows(rx, ry, rz, lo=0, hi=own):
        return pl.ds(((rx * ny + ry) * nz + rz) * own + lo, hi - lo)

    pending = []

    def launch(copy):
        copy.start()
        pending.append(copy)
        return copy

    z_in = {
        k: launch(send(tok.at[rows(0, 0, 0)], tok.at[rows(0, 0, k)], at(dz=-k)))
        for k in range(1, nz)
    }
    x_in, y_in, xy_in = {}, {}, {}

    def forward_x(ry, rz):
        for k in range(1, nx):
            hi = cut if ry else own
            x_in[k, ry, rz] = launch(
                send(tok.at[rows(0, ry, rz, 0, hi)], tok.at[rows(k, ry, rz, 0, hi)], at(dx=-k))
            )

    def forward_xy(k, rz):
        if cut == own:
            return
        for ky in range(1, ny):
            xy_in[k, ky, rz] = launch(
                send(
                    tok.at[rows(k, 0, rz, cut)], tok.at[rows(k, ky, rz, cut)], at(dy=-ky)
                )
            )

    def forward_y(rz):
        for k in range(1, ny):
            y_in[k, rz] = launch(
                send(tok.at[rows(0, 0, rz)], tok.at[rows(0, k, rz)], at(dy=-k))
            )

    forward_x(0, 0)
    forward_y(0)
    everyone = jnp.broadcast_to(tgt_ref[...], (8, nz * ny * own))
    lane = lax.broadcasted_iota(jnp.int32, (8, nz * ny * own), 1)
    for ry in range(ny):
        line = everyone
        for rz in range(nz):
            owner = lax.rem(z + rz, nz) * ny + lax.rem(y + ry, ny)
            turn = lax.rem(rz - owner + nz * ny, nz * ny) * own
            line = jnp.where(lane >= rz * own, pltpu.roll(everyone, turn, 1), line) if rz else (
                pltpu.roll(everyone, turn, 1)
            )
        tg[ry] = line[0:1, 0:wide]
    tg_in = {
        k: launch(send(tg.at[pl.ds(0, ny)], tg.at[pl.ds(k * ny, ny)], at(dx=-k)))
        for k in range(1, nx)
    }
    for rz in range(1, nz):
        z_in[rz].wait_recv()
        forward_x(0, rz)
        forward_y(rz)
    for load in loads:
        load.wait()

    nt = (((1,), (1,)), ((), ()))

    def base_of(b):
        return jnp.where(b < half_blocks, bases[0] + b * kb, bases[1] + (b - half_blocks) * kb)

    def hits(g, b):
        ids = lax.broadcasted_iota(jnp.int32, (kb, wide), 0)
        return ids == (tg[g] - base_of(b))

    def first_pass(g):
        lat_g = tok[g * wide : (g + 1) * wide, 0:width]
        grad_g = tok[g * wide : (g + 1) * wide, width:]

        def body(b, carry):
            here = pl.ds(pl.multiple_of(b * kb, kb), kb)
            part = book[here, :]
            logit = lax.dot_general(part, lat_g, nt, preferred_element_type=F32)
            bk = lax.dot_general(part, grad_g, nt, preferred_element_type=F32)
            top = jnp.max(logit, axis=0, keepdims=True)
            ex = jnp.exp(logit - top)
            expo[g, here, :] = ex
            back[g, here, :] = bk
            tops[g, pl.ds(b, 1), :] = top
            sums[0, pl.ds(b, 1), :] = jnp.sum(ex, axis=0, keepdims=True)
            sums[1, pl.ds(b, 1), :] = jnp.sum(ex * bk, axis=0, keepdims=True)
            sums[2, pl.ds(b, 1), :] = jnp.sum(
                jnp.where(hits(g, b), logit, 0.0), axis=0, keepdims=True
            )
            return carry

        lax.fori_loop(0, blocks, body, 0, unroll=2)
        block_tops = tops[g]
        top = jnp.max(block_tops, axis=0, keepdims=True)
        factor = jnp.exp(block_tops - top)
        stats[0, g, 0:1, :] = top
        stats[0, g, 1:2, :] = jnp.sum(sums[0] * factor, axis=0, keepdims=True)
        stats[0, g, 2:3, :] = jnp.sum(sums[1] * factor, axis=0, keepdims=True)
        stats[0, g, 3:4, :] = jnp.sum(sums[2], axis=0, keepdims=True)

    first_pass(0)
    for k in range(1, ny):
        for rz in range(nz):
            y_in[k, rz].wait_recv()
            forward_x(k, rz)
    for k in range(1, nx):
        for rz in range(nz):
            x_in[k, 0, rz].wait_recv()
            forward_xy(k, rz)
    for ry in range(1, ny):
        first_pass(ry)
    for b in range(blocks):
        book_t[:, b * kb : (b + 1) * kb] = book[b * kb : (b + 1) * kb, :].T
    for k in range(1, nx):
        tg_in[k].wait_recv()
        for ry in range(ny):
            for rz in range(nz):
                if ry:
                    x_in[k, ry, rz].wait_recv()
                    if cut < own:
                        xy_in[k, ry, rz].wait_recv()
            first_pass(k * ny + ry)

    def merge(mine, theirs):
        top = jnp.maximum(mine[0:1], theirs[0:1])
        fm, ft = jnp.exp(mine[0:1] - top), jnp.exp(theirs[0:1] - top)
        return jnp.concatenate(
            [
                top,
                mine[1:2] * fm + theirs[1:2] * ft,
                mine[2:3] * fm + theirs[2:3] * ft,
                mine[3:4] + theirs[3:4],
            ],
            axis=0,
        )

    def direct_part(lo, hi):
        def body(b, carry):
            here = pl.ds(pl.multiple_of(b * kb, kb), kb)
            total = None
            for g in range(groups):
                onehot = hits(g, b).astype(F32).astype(BF16)
                term = jnp.dot(
                    onehot, tok[g * wide : (g + 1) * wide, width:], preferred_element_type=F32
                )
                total = term if total is None else total + term
            if lo == 0:
                other[here, :] = total
            else:
                same[pl.ds(pl.multiple_of((b - half_blocks) * kb, kb), kb), :] = total
            return carry

        lax.fori_loop(lo, hi, body, 0)

    slot = 0
    stages = [square, [(k,) for k in range(1, nz)]]
    for s, peers in enumerate(stages):
        arrivals = []
        for peer in peers:
            to = at(-peer[0], -peer[1]) if s == 0 else at(dz=-peer[0])
            copy = launch(send(stats.at[s], stats_in.at[slot], to))
            arrivals.append((peer, slot, copy))
            slot += 1
        if s == 0:
            direct_part(0, half_blocks)
        else:
            direct_part(half_blocks, blocks)
        for _, _, copy in arrivals:
            copy.wait_recv()
        for g in range(groups):
            rx, ry = g // ny, g % ny
            value = stats[s, g]
            for peer, place, _ in arrivals:
                if s == 0:
                    theirs = stats_in[place, ((rx - peer[0]) % nx) * ny + (ry - peer[1]) % ny]
                else:
                    theirs = pltpu.roll(stats_in[place, g], peer[0] * own, 1)
                value = merge(value, theirs)
            stats[s + 1, g] = value
    final = len(stages)
    top = stats[final, 0, 0:1, :]
    loss = top + jnp.log(stats[final, 0, 1:2, :]) - stats[final, 0, 3:4, :]
    loss_ref[...] = loss[:, 0:own]

    def second_pass(g):
        lse = stats[final, g, 0:1, :] + jnp.log(stats[final, g, 1:2, :])
        shift = 1.0 - stats[final, g, 2:3, :] / stats[final, g, 1:2, :]
        acc[...] = jnp.zeros_like(acc)

        def body(b, carry):
            here = pl.ds(pl.multiple_of(b * kb, kb), kb)
            scale = jnp.exp(tops[g, pl.ds(b, 1), :] - lse)
            probs = expo[g, here, :] * scale
            value = probs * (back[g, here, :] + shift)
            value = value - jnp.where(hits(g, b), 1.0, 0.0)
            value = value.astype(BF16)
            delta[here, g * wide : (g + 1) * wide] = value
            acc[...] += jnp.dot(book_t[:, here], value, preferred_element_type=F32)
            return carry

        lax.fori_loop(0, blocks, body, 0, unroll=2)
        lgrad[g * wide : (g + 1) * wide, :] = acc[...].T.astype(BF16)

    lx_in, ly_in, lz_in = {}, {}, {}
    for k in range(1, nx):
        for ry in reversed(range(ny)):
            g = k * ny + ry
            second_pass(g)
            lx_in[k, ry] = launch(
                send(
                    lgrad.at[pl.ds(g * wide, wide)],
                    lgrad_x.at[pl.ds(((k - 1) * ny + ry) * wide, wide)],
                    at(dx=k),
                )
            )
    for ry in reversed(range(ny)):
        second_pass(ry)

    def sum_x(ry):
        value = lgrad[ry * wide : (ry + 1) * wide, :].astype(F32)
        for k in range(1, nx):
            lx_in[k, ry].wait_recv()
            value += lgrad_x[((k - 1) * ny + ry) * wide : ((k - 1) * ny + ry + 1) * wide, :].astype(F32)
        return value

    other_copies = []
    for b in range(half_blocks):
        here = pl.ds(b * kb, kb)
        other[here, :] += jnp.dot(delta[b * kb : (b + 1) * kb, :], tok[:, 0:width], preferred_element_type=F32)
        other_copies.append(launch(send(other.at[here], theirs_ref.at[here], mate)))

    for k in range(1, ny):
        lgrad[k * wide : (k + 1) * wide, :] = sum_x(k).astype(BF16)
        ly_in[k] = launch(
            send(
                lgrad.at[pl.ds(k * wide, wide)],
                lgrad_y.at[pl.ds((k - 1) * wide, wide)],
                at(dy=k),
            )
        )
    mine = sum_x(0)
    acc[...] = mine
    stores = []
    for b in range(half_blocks):
        here = pl.ds(b * kb, kb)
        same[here, :] += jnp.dot(
            delta[sub + b * kb : sub + (b + 1) * kb, :], tok[:, 0:width], preferred_element_type=F32
        )
        store = pltpu.make_async_copy(same.at[here], mine_ref.at[here], lsem.at[2 + b])
        store.start()
        stores.append(store)

    mine = acc[...]
    for k in range(1, ny):
        ly_in[k].wait_recv()
        mine = mine + lgrad_y[(k - 1) * wide : k * wide, :].astype(F32)
    acc[...] = mine
    for k in range(1, nz):
        lz_in[k] = launch(
            send(
                acc.at[pl.ds(k * own, own)],
                lgrad_z.at[pl.ds((k - 1) * own, own)],
                at(dz=k),
            )
        )
    for b in range(half_blocks):
        other_copies[b].wait_recv()
        stores[b].wait()
    mine = acc[0:own, :]
    for k in range(1, nz):
        lz_in[k].wait_recv()
        mine = mine + lgrad_z[(k - 1) * own : k * own, :]
    lg_ref[...] = mine.astype(BF16)
    for copy in pending:
        copy.wait_send()


def per_device(latents, out_grad, targets, codebook):
    own, width = latents.shape
    code_dev = codebook.shape[0]
    dp, code = lax.axis_size("dp"), lax.axis_size("code")
    nx, ny, nz = dims_of(dp, code)
    groups = nx * ny
    wide = nz * own
    sub = code_dev // dp
    codes = CORES * sub
    kb = min(512, sub)
    blocks = codes // kb
    tokens = groups * wide

    copies = (nz - 1) + (nx - 1) * (ny * nz + 1) + (ny - 1) * nz
    copies += (nx * ny - 1) + (nz - 1) + (nx - 1) * (ny - 1) * nz
    copies += (nx - 1) * ny + (ny - 1) + (nz - 1) + sub // kb
    vmem = pl.BlockSpec(memory_space=pltpu.VMEM)
    macs = tokens * codes * width
    lat_out, mine, theirs, loss = pl.pallas_call(
        functools.partial(kernel, (nx, ny, nz, kb)),
        out_shape=(
            jax.ShapeDtypeStruct((own, width), BF16),
            jax.ShapeDtypeStruct((sub, width), F32),
            jax.ShapeDtypeStruct((sub, width), F32),
            jax.ShapeDtypeStruct((1, own), F32),
        ),
        in_specs=[vmem, vmem, vmem, pl.BlockSpec(memory_space=pl.ANY)],
        out_specs=(vmem, pl.BlockSpec(memory_space=pl.ANY), pl.BlockSpec(memory_space=pl.ANY), vmem),
        scratch_shapes=[
            pltpu.VMEM((tokens, 2 * width), BF16),
            pltpu.VMEM((groups, 1, wide), jnp.int32),
            pltpu.VMEM((codes, width), BF16),
            pltpu.VMEM((width, codes), BF16),
            pltpu.VMEM((groups, codes, wide), F32),
            pltpu.VMEM((groups, codes, wide), F32),
            pltpu.VMEM((codes, tokens), BF16),
            pltpu.VMEM((groups, blocks, wide), F32),
            pltpu.VMEM((3, blocks, wide), F32),
            pltpu.VMEM((3, groups, 4, wide), F32),
            pltpu.VMEM((max(1, nx * ny + nz - 2), groups, 4, wide), F32),
            pltpu.VMEM((sub, width), F32),
            pltpu.VMEM((sub, width), F32),
            pltpu.VMEM((tokens, width), BF16),
            pltpu.VMEM((max(1, nx - 1) * ny * wide, width), BF16),
            pltpu.VMEM((max(1, ny - 1) * wide, width), BF16),
            pltpu.VMEM((max(1, nz - 1) * own, width), F32),
            pltpu.VMEM((width, wide), F32),
            pltpu.SemaphoreType.DMA((copies,)),
            pltpu.SemaphoreType.DMA((copies,)),
            pltpu.SemaphoreType.DMA((2 + sub // kb,)),
        ],
        compiler_params=pltpu.CompilerParams(
            collective_id=0, has_side_effects=True, vmem_limit_bytes=62 * 2**20
        ),
        cost_estimate=pl.CostEstimate(
            flops=10 * macs, bytes_accessed=2 * codes * width, transcendentals=tokens * codes
        ),
    )(latents, out_grad, targets.reshape(1, -1), codebook)

    def finish(lat_ref, mine_ref, theirs_ref, loss_ref, lat_to, book_to, loss_to):
        book_to[...] = mine_ref[...] + theirs_ref[...]
        lat_to[...] = lat_ref[...]
        loss_to[...] = loss_ref[0, :]

    whole_lat = pl.BlockSpec((own, width), lambda i: (0, 0))
    tile = pl.BlockSpec((kb, width), lambda i: (i, 0))
    return pl.pallas_call(
        finish,
        grid=(sub // kb,),
        out_shape=(
            jax.ShapeDtypeStruct((own, width), BF16),
            jax.ShapeDtypeStruct((sub, width), F32),
            jax.ShapeDtypeStruct((own,), F32),
        ),
        in_specs=[whole_lat, tile, tile, pl.BlockSpec((1, own), lambda i: (0, 0))],
        out_specs=(whole_lat, tile, pl.BlockSpec((own,), lambda i: (0,))),
    )(lat_out, mine, theirs, loss)


def solution(mesh):
    in_specs = (P(("dp", "code"), None), P(("dp", "code"), None), P("dp"), P("code", None))
    out_specs = (P(("dp", "code"), None), P(("code", "dp"), None), P(("dp", "code")))
    return jax.shard_map(
        per_device, mesh=mesh, in_specs=in_specs, out_specs=out_specs, check_vma=False
    )
```
